128 devices in a mesh: dp: 16 (over z_hi, x, core), tensor: 8 (over y, z_lo).
Axes of the slice: x: 4, y: 4, z: 4 (z_hi: 2, z_lo: 2; z = z_hi * 2 + z_lo), core: 2. Of those that a mesh axis runs over, the one named last changes fastest.
Arguments:
- train_hidden: bfloat16 [32768, 28672], P('dp', 'tensor'), may hold values from -6 to 6
- train_grad: bfloat16 [32768, 8192], P('dp', 'tensor'), may hold values from -6 to 6
- val_hidden: bfloat16 [1024, 28672], P('dp', 'tensor'), may hold values from -6 to 6
- val_grad: bfloat16 [1024, 8192], P('dp', 'tensor'), may hold values from -6 to 6
- seq_ids: int32 [16, 2048], P('dp'), may hold values from 0 to 7, never falling along the last dimension, each value on 1 to 1024 neighbouring positions
Outputs:
- seq_scores: float32 [128], P('dp')
- val_scores: float32 [1024], replicated
The draws below stay inside these ranges and needn't reach their ends.
Inputs may be any that keep to these rules, and one draw needn't show every extreme that they name: Each row of seq_ids does not decrease, names every number 0 to 7, and no number more than 1024 times.
All inputs are finite; a program needn't handle non-finite values.
Results may differ from the reference program's by a relative error of at most 0.0003.
Values may be sent and summed in bfloat16 or wider, within the bound.
No kernel may reach another device: no remote copies, remote signals or barrier semaphores. Data moves between devices by JAX's collectives and lax.ppermute only.
A program may use at most 128 MiB of HBM per device.

```python
import math
import jax
import jax.numpy as jnp
import numpy as np
from jax import lax

D = 8192
FF = 28672
TOK_DEV = 2048
SEQ_DEV = 8
VAL = 1024
BLOCKS = 16
MOST = 1024
TOKENS = 32768


def levels(key, dims, pieces, low, largest):
    def one(position, parts):
        heights = jax.random.uniform(jax.random.fold_in(jax.random.fold_in(key, 6), position), (parts,), jnp.float32, low / len(pieces), largest / len(pieces))
        return jnp.repeat(jnp.exp(heights), dims[position] // parts).reshape((-1,) + (1,) * (len(dims) - position - 1))

    factor_of = one(*pieces[0])
    for cut in pieces[1:]:
        factor_of = factor_of * one(*cut)
    return factor_of


def profile(count, total, bound, lean):
    weights = [(1 << 20) // math.isqrt(standing ** lean) + 1 for standing in range(2, count + 1)]
    surplus, holding = total - bound - (count - 1), [1] * (count - 1)
    while surplus > 0:
        movable = [i for i in range(count - 1) if holding[i] < bound]
        pool, left = sum([weights[i] for i in movable]), surplus
        for i in movable:
            addition = min(bound - holding[i], max(1, left * weights[i] // pool), surplus)
            holding[i] = holding[i] + addition
            surplus = surplus - addition
    return np.array([bound] + holding)


def ragged(own_key, number_of, total, reach, skew):
    if number_of == 2:
        one = jax.random.randint(own_key, (), max(1, total - reach), min(reach, total - 1) + 1)
        return jnp.stack([one, total - one])
    lengths = jnp.asarray(profile(number_of, total, reach, skew), jnp.int32)
    pairs = (number_of - 1) // 2
    source_of, sink = lengths[1:1 + 2 * pairs:2], lengths[2:2 + 2 * pairs:2]
    slack = jnp.minimum(source_of - 1, reach - sink)
    passed = jax.random.randint(jax.random.fold_in(own_key, 1), (pairs,), 0, 1 << 20) % (slack + 1)
    lengths = lengths.at[1:1 + 2 * pairs:2].set(source_of - passed).at[2:2 + 2 * pairs:2].set(sink + passed)
    return lengths[jax.random.permutation(jax.random.fold_in(own_key, 2), number_of)]


def noise(own_key, extent, scale, most, split=(), dtype=jnp.bfloat16):
    drawn = jax.random.normal(own_key, extent, jnp.float32) * scale
    if len(split) > 0:
        drawn = levels(own_key, extent, split, -0.22, 0.18) * drawn
    return jnp.clip(drawn, min=-most, max=most).astype(dtype)


def setup_inputs(seed: int = 0) -> dict:
    keys = jax.random.split(jax.random.key(seed), 6)
    return {
        "train_hidden": noise(keys[0], (TOKENS, FF), 1.0, 6.0, ((0, 16), (1, 8))),
        "train_grad": noise(keys[1], (TOKENS, D), 1.0, 6.0, ((0, 16), (1, 8))),
        "val_hidden": noise(keys[2], (VAL, FF), 1.0, 6.0, ((0, 16), (1, 8))),
        "val_grad": noise(keys[3], (VAL, D), 1.0, 6.0, ((0, 16), (1, 8))),
        "seq_ids": jax.vmap(lambda own: jnp.searchsorted(jnp.cumsum(ragged(own, SEQ_DEV, TOK_DEV, MOST, 2)), jnp.arange(TOK_DEV), side="right"))(jax.random.split(keys[4], BLOCKS)).reshape((BLOCKS, TOK_DEV)).astype(jnp.int32),
    }


def reference(train_hidden, train_grad, val_hidden, val_grad, seq_ids):
    hidden_blocks = train_hidden.reshape(BLOCKS, TOK_DEV, FF)
    grad_blocks = train_grad.reshape(BLOCKS, TOK_DEV, D)
    labels = jnp.arange(SEQ_DEV).astype(jnp.int32)

    def step(total, items):
        hidden, grads, ids = items
        act_gram = jnp.dot(hidden, val_hidden.T, preferred_element_type=jnp.float32)
        grad_gram = jnp.dot(grads, val_grad.T, preferred_element_type=jnp.float32)
        ghost = act_gram * grad_gram
        row_sums = jnp.sum(ghost, axis=1)
        member = ids.astype(jnp.int32)[:, None] == labels[None, :]
        segment = jnp.sum(jnp.where(member, row_sums[:, None], jnp.zeros_like(row_sums)[:, None]), axis=0)
        return total + jnp.sum(ghost, axis=0), segment

    total, segments = lax.scan(step, jnp.zeros((VAL,), jnp.float32), (hidden_blocks, grad_blocks, seq_ids))
    seq_scores = segments.reshape(-1) * (1.0 / (float(FF) * D * VAL * TOK_DEV) ** 0.5)
    val_scores = total * (1.0 / (float(FF) * D * TOKENS) ** 0.5)
    return seq_scores, val_scores
```

```python
import jax
import jax.numpy as jnp
import numpy as np
from jax import lax
from jax.experimental import pallas as pl
from jax.experimental.pallas import tpu as pltpu
from jax.sharding import PartitionSpec as P

D = 8192
FF = 28672
TOK_DEV = 2048
SEQ_DEV = 8
VAL = 1024

DP = 16
TENSOR = 8
VAL_DEV = VAL // DP
HALF = VAL // 2
LEAF = TOK_DEV // TENSOR
GROUP = 64
BIAS = 100.0
MANTISSA = 16383.0
VMEM = 56 * 1024 * 1024


def along_z(d):
    return (d + 8) % 16


def along_core(d):
    return d ^ 1


def move_x(d, fn):
    z, x, core = d // 8, d // 2 % 4, d % 2
    return z * 8 + fn(x) * 2 + core


def first_x(d):
    return move_x(d, lambda x: x ^ 1 if d % 2 == 0 else 3 - x)


def second_x(d):
    return move_x(d, lambda x: 3 - x if d % 2 == 0 else x ^ 1)


def along_link(t, link):
    y, z = t // 2, t % 2
    if link == 0:
        return (y ^ 1) * 2 + z
    if link == 1:
        return (3 - y) * 2 + z
    return t ^ 1


ORDER = (((0, 1, 2), (2, 0, 1)), ((1, 0, 2), (2, 1, 0)))


def send_dp(x, fn):
    return lax.ppermute(x, "dp", [(d, fn(d)) for d in range(DP)])


def send_link(x, group, step):
    pairs = []
    for d in range(DP):
        link = ORDER[d % 2][group][step]
        for t in range(TENSOR):
            pairs.append((d * TENSOR + t, d * TENSOR + along_link(t, link)))
    return lax.ppermute(x, ("dp", "tensor"), pairs)


def send_wrap(x):
    pairs = []
    for d in range(DP):
        for t in range(TENSOR):
            pairs.append((d * TENSOR + t, along_z(d) * TENSOR + (t ^ 1)))
    return lax.ppermute(x, ("dp", "tensor"), pairs)


def gather(rows):
    pair = jnp.concatenate([rows, send_dp(rows, along_z)])
    quad = jnp.concatenate([pair, send_dp(pair, first_x)])
    own = jnp.concatenate([quad, send_dp(quad, second_x)])
    return own, send_dp(own, along_core)


def gather_order():
    held = [[d] for d in range(DP)]
    for fn in (along_z, first_x, second_x, along_core):
        held = [held[d] + held[fn(d)] for d in range(DP)]
    return np.array(held, np.int32)


def encode(x):
    a = x.reshape(8, 8, x.shape[-1])
    top = jnp.max(jnp.abs(a), axis=0)
    e = jnp.clip(jnp.floor(jnp.log2(jnp.maximum(top, 1e-26)) + 1.0002), -90.0, 120.0)
    inv = jnp.exp2(-e) * MANTISSA
    code = (e + BIAS).astype(jnp.int32)
    q = jnp.floor(a * inv[None] + 0.5).astype(jnp.int32) * 2
    bits = jnp.stack([(code >> i) & 1 for i in range(8)])
    return (q + bits).reshape(x.shape).astype(jnp.int16)


def decode(c):
    c = c.astype(jnp.int32).reshape(8, 8, c.shape[-1])
    low = c & 1
    code = low[0]
    for i in range(1, 8):
        code = code | (low[i] << i)
    s = jnp.exp2(code.astype(jnp.float32) - BIAS) * (1.0 / MANTISSA)
    return ((c >> 1).astype(jnp.float32) * s[None]).reshape(GROUP, c.shape[-1])


def tiles(m, n):
    for r in range(0, m, GROUP):
        for c in range(0, n, 128):
            yield slice(r, r + GROUP), slice(c, c + 128)


def gram(x, y, half, coded, block=512):
    n, k = y.shape
    rows = TOK_DEV // 2
    nb = rows // block

    def kernel(half_ref, x_ref, y_ref, o_ref):
        acc = lax.dot_general(
            x_ref[...], y_ref[...], (((1,), (1,)), ((), ())), preferred_element_type=jnp.float32
        )
        if coded:
            for r, c in tiles(block, n):
                o_ref[r, c] = encode(acc[r, c])
        else:
            o_ref[...] = acc

    return pl.pallas_call(
        kernel,
        out_shape=jax.ShapeDtypeStruct((rows, n), jnp.int16 if coded else jnp.float32),
        grid_spec=pltpu.PrefetchScalarGridSpec(
            num_scalar_prefetch=1,
            grid=(nb,),
            in_specs=[
                pl.BlockSpec((block, k), lambda i, h: (h[0] * nb + i, 0)),
                pl.BlockSpec((n, k), lambda i, h: (0, 0)),
            ],
            out_specs=pl.BlockSpec((block, n), lambda i, h: (i, 0)),
        ),
        compiler_params=pltpu.CompilerParams(vmem_limit_bytes=VMEM),
        cost_estimate=pl.CostEstimate(
            flops=2 * rows * n * k, bytes_accessed=2 * (rows + n) * k + 4 * rows * n, transcendentals=0
        ),
        name="gram",
    )(half, x, y)


def fold(kept, arrived, keep):
    rows, n = kept.shape
    block = 256
    nb = rows // 2 // block

    def kernel(keep_ref, ks_ref, as_ref, kk_ref, ak_ref, send_ref, kept_ref):
        for r, c in tiles(block, n):
            send_ref[r, c] = encode(ks_ref[r, c] + decode(as_ref[r, c]))
        for r, c in tiles(block, n):
            kept_ref[r, c] = kk_ref[r, c] + decode(ak_ref[r, c])

    away = pl.BlockSpec((block, n), lambda i, k: ((1 - k[0]) * nb + i, 0))
    stay = pl.BlockSpec((block, n), lambda i, k: (k[0] * nb + i, 0))
    out = pl.BlockSpec((block, n), lambda i, k: (i, 0))
    return pl.pallas_call(
        kernel,
        out_shape=(
            jax.ShapeDtypeStruct((rows // 2, n), jnp.int16),
            jax.ShapeDtypeStruct((rows // 2, n), jnp.float32),
        ),
        grid_spec=pltpu.PrefetchScalarGridSpec(
            num_scalar_prefetch=1,
            grid=(nb,),
            in_specs=[away, away, stay, stay],
            out_specs=(out, out),
        ),
        compiler_params=pltpu.CompilerParams(vmem_limit_bytes=VMEM),
        cost_estimate=pl.CostEstimate(flops=40 * rows * n, bytes_accessed=9 * rows * n, transcendentals=0),
        name="fold",
    )(keep, kept, arrived, kept, arrived)


def finish(act, act_in, grad, grad_in, ids, leaf):
    n = act.shape[1]

    def kernel(leaf_ref, a_ref, ai_ref, g_ref, gi_ref, ids_ref, col_ref, seq_ref):
        lane = lax.broadcasted_iota(jnp.int32, (GROUP, 128), 1)
        seq = jnp.zeros((1, 128), jnp.float32)
        cols = [jnp.zeros((1, 128), jnp.float32) for _ in range(n // 128)]
        for r in range(0, LEAF, GROUP):
            rows = slice(r, r + GROUP)
            wide = jnp.zeros((GROUP, 128), jnp.float32)
            for j in range(n // 128):
                c = slice(j * 128, j * 128 + 128)
                ghost = (a_ref[rows, c] + decode(ai_ref[rows, c])) * (g_ref[rows, c] + decode(gi_ref[rows, c]))
                wide = wide + ghost
                cols[j] = cols[j] + jnp.sum(ghost, axis=0, keepdims=True)
            total = jnp.sum(wide, axis=1, keepdims=True)
            seq = seq + jnp.sum(jnp.where(ids_ref[rows] == lane, total, 0.0), axis=0, keepdims=True)
        for j in range(n // 128):
            col_ref[:, j * 128 : j * 128 + 128] = cols[j]
        seq_ref[...] = seq

    whole = pl.BlockSpec((LEAF, n), lambda i, s: (0, 0))
    return pl.pallas_call(
        kernel,
        out_shape=(jax.ShapeDtypeStruct((1, n), jnp.float32), jax.ShapeDtypeStruct((1, 128), jnp.float32)),
        grid_spec=pltpu.PrefetchScalarGridSpec(
            num_scalar_prefetch=1,
            grid=(1,),
            in_specs=[whole, whole, whole, whole, pl.BlockSpec((LEAF, 1), lambda i, s: (s[0], 0))],
            out_specs=(pl.BlockSpec((1, n), lambda i, s: (0, 0)), pl.BlockSpec((1, 128), lambda i, s: (0, 0))),
        ),
        compiler_params=pltpu.CompilerParams(vmem_limit_bytes=VMEM),
        cost_estimate=pl.CostEstimate(flops=40 * LEAF * n, bytes_accessed=12 * LEAF * n, transcendentals=0),
        name="finish",
    )(leaf, act, act_in, grad, grad_in, ids)


def local(train_hidden, train_grad, val_hidden, val_grad, seq_ids):
    ids = seq_ids.reshape(TOK_DEV, 1)
    d = lax.axis_index("dp")
    t = lax.axis_index("tensor")
    core = d % 2
    y, z = t // 2, t % 2
    bits = jnp.stack([((y + 1) // 2) % 2, y // 2, z]).astype(jnp.int32)
    order = jnp.asarray(np.array(ORDER, np.int32))[core]

    def bit(group, step):
        return bits[order[group, step]].reshape(1)

    def halve(x, vals, group):
        keep = bit(group, 0)
        arrived = send_link(gram(x, vals, 1 - keep, True), group, 0)
        kept = gram(x, vals, keep, False)
        for step in (1, 2):
            send, kept = fold(kept, arrived, bit(group, step))
            arrived = send_link(send, group, step)
        return kept, arrived

    grads = gather(val_grad)
    acts = gather(val_hidden)
    grad_parts = [halve(train_grad, grads[g], g) for g in range(2)]
    act_parts = [halve(train_hidden, acts[g], g) for g in range(2)]

    cols, seqs = [], []
    for g in range(2):
        leaf = bit(g, 0) * 4 + bit(g, 1) * 2 + bit(g, 2)
        col, seq = finish(*act_parts[g], *grad_parts[g], ids, leaf)
        cols.append(col)
        seqs.append(seq)
    place = jnp.asarray(gather_order())[d]
    ours = (place[None, :] == jnp.arange(DP, dtype=jnp.int32)[:, None])[:, :, None]
    col = jnp.concatenate(cols, axis=1).reshape(1, DP, VAL_DEV)
    col = jnp.sum(jnp.where(ours, col, 0.0), axis=1).reshape(8, 128)
    total = jnp.concatenate([col, seqs[0] + seqs[1]], axis=0)
    for link in range(3):
        total = total + lax.ppermute(total, "tensor", [(i, along_link(i, link)) for i in range(TENSOR)])
    segment = total[8, :SEQ_DEV]
    total = total[:8]
    for fn in (first_x, second_x):
        total = total + send_dp(total, fn)
    total = total + send_wrap(total)
    total = total + send_dp(total, along_core)
    seq_scale = 1.0 / (float(FF) * D * VAL * TOK_DEV) ** 0.5
    val_scale = 1.0 / (float(FF) * D * TOK_DEV * DP) ** 0.5
    return (segment * seq_scale, total.reshape(VAL) * val_scale)


def solution(mesh):
    in_specs = (
        P("dp", "tensor"),
        P("dp", "tensor"),
        P("dp", "tensor"),
        P("dp", "tensor"),
        P("dp", None),
    )
    out_specs = (P("dp"), P())
    return jax.shard_map(local, mesh=mesh, in_specs=in_specs, out_specs=out_specs, check_vma=False)
```

```python
import jax
import jax.numpy as jnp
import numpy as np
from jax import lax
from jax.experimental import pallas as pl
from jax.experimental.pallas import tpu as pltpu
from jax.sharding import PartitionSpec as P

D = 8192
FF = 28672
TOK_DEV = 2048
SEQ_DEV = 8
VAL = 1024

DP = 16
TENSOR = 8
VAL_DEV = VAL // DP
LEAF = TOK_DEV // TENSOR
WAVE = VAL // 2
HIDDEN_DEV = FF // TENSOR
GRAD_DEV = D // TENSOR
GROUP = 64
BIAS = 100.0
MANTISSA = 16383.0


def along_z(d):
    return (d + 8) % 16


def along_core(d):
    return d ^ 1


def move_x(d, fn):
    z, x, core = d // 8, d // 2 % 4, d % 2
    return z * 8 + fn(x) * 2 + core


def first_x(d):
    return move_x(d, lambda x: x ^ 1 if d % 2 == 0 else 3 - x)


def second_x(d):
    return move_x(d, lambda x: 3 - x if d % 2 == 0 else x ^ 1)


def along_link(t, link):
    y, z = t // 2, t % 2
    if link == 0:
        return (y ^ 1) * 2 + z
    if link == 1:
        return (3 - y) * 2 + z
    return t ^ 1


LINK_OF_BIT = ((0, 1, 2), (1, 0, 2))


def send_dp(x, fn):
    return lax.ppermute(x, "dp", [(d, fn(d)) for d in range(DP)])


def send_link(x, bit):
    pairs = []
    for d in range(DP):
        link = LINK_OF_BIT[d % 2][bit]
        for t in range(TENSOR):
            pairs.append((d * TENSOR + t, d * TENSOR + along_link(t, link)))
    return lax.ppermute(x, ("dp", "tensor"), pairs)


def send_wrap(x):
    pairs = []
    for d in range(DP):
        for t in range(TENSOR):
            pairs.append((d * TENSOR + t, along_z(d) * TENSOR + (t ^ 1)))
    return lax.ppermute(x, ("dp", "tensor"), pairs)


def encode(x):
    a = x.reshape(8, 8, x.shape[-1])
    top = jnp.max(jnp.abs(a), axis=0)
    e = jnp.clip(jnp.floor(jnp.log2(jnp.maximum(top, 1e-26)) + 1.0002), -90.0, 120.0)
    inv = jnp.exp2(-e) * MANTISSA
    code = (e + BIAS).astype(jnp.int32)
    q = jnp.floor(a * inv[None] + 0.5).astype(jnp.int32) * 2
    bits = jnp.stack([(code >> i) & 1 for i in range(8)])
    return (q + bits).reshape(x.shape).astype(jnp.int16)


def decode(c):
    c = c.astype(jnp.int32).reshape(8, 8, c.shape[-1])
    low = c & 1
    code = low[0]
    for i in range(1, 8):
        code = code | (low[i] << i)
    s = jnp.exp2(code.astype(jnp.float32) - BIAS) * (1.0 / MANTISSA)
    return ((c >> 1).astype(jnp.float32) * s[None]).reshape(GROUP, c.shape[-1])


IN_VMEM = pl.BlockSpec(memory_space=pltpu.VMEM)
IN_SMEM = pl.BlockSpec(memory_space=pltpu.SMEM)
IN_HBM = pl.BlockSpec(memory_space=pltpu.HBM)
BRIEF = pl.CostEstimate(flops=1, bytes_accessed=1, transcendentals=0)


def vmem(x):
    return pltpu.with_memory_space_constraint(x, pltpu.VMEM)


def params(mib):
    return pltpu.CompilerParams(vmem_limit_bytes=mib * 1024 * 1024)


def part(start, size):
    if isinstance(start, int):
        return pl.ds(start, size)
    return pl.ds(pl.multiple_of(start, size), size)


def join(arrays):
    rows = [a.shape[0] for a in arrays]
    n = arrays[0].shape[1]

    def kernel(*refs):
        to = 0
        for ref, size in zip(refs[:-1], rows):
            refs[-1][to : to + size] = ref[...]
            to += size

    return pl.pallas_call(
        kernel,
        out_shape=pltpu.VMEM((sum(rows), n), arrays[0].dtype),
        in_specs=[IN_VMEM] * len(arrays),
        out_specs=IN_VMEM,
        compiler_params=params(4),
        cost_estimate=BRIEF,
        name="join",
    )(*[vmem(a) for a in arrays])


def beside(hidden, grad):
    def kernel(hidden_ref, grad_ref, out_ref):
        out_ref[:, :HIDDEN_DEV] = hidden_ref[...]
        out_ref[:, HIDDEN_DEV:] = grad_ref[...]

    return pl.pallas_call(
        kernel,
        out_shape=pltpu.VMEM((VAL_DEV, HIDDEN_DEV + GRAD_DEV), hidden.dtype),
        in_specs=[IN_VMEM, IN_VMEM],
        out_specs=IN_VMEM,
        compiler_params=params(4),
        cost_estimate=BRIEF,
        name="beside",
    )(vmem(hidden), vmem(grad))


def tie(x, after):
    return lax.optimization_barrier((x, after))[0]


def pieces(rows, count, fn):
    size = rows.shape[0] // count
    return [send_dp(rows[i * size : (i + 1) * size], fn) for i in range(count)]


def both_cores(twice):
    groups = [[d, d + 1] for d in range(0, DP, 2)]
    return lax.all_to_all(twice, "dp", 0, 0, axis_index_groups=groups, tiled=True)


def column_order(d):
    order = []
    for far in (False, True):
        near_part, other_part = [], []
        for e, held in ((d, near_part), (along_core(d), other_part)):
            e = along_z(e) if far else e
            held += [e, first_x(e), second_x(e), first_x(second_x(e))]
        rest = (near_part[2:], other_part[2:])
        rest = rest[:: -1 if far and d % 2 else 1]
        order += near_part[:2] + other_part[:2] + rest[0] + rest[1]
    return order


def gram(scalars, x, y, bit, away):
    n, k = y.shape[0], x.shape[1]
    columns = slice(0, HIDDEN_DEV) if k == HIDDEN_DEV else slice(HIDDEN_DEV, HIDDEN_DEV + GRAD_DEV)
    rows = TOK_DEV // 2
    low = 2 - bit
    streamed = False

    def kernel(s_ref, x_ref, y_ref, o_ref, acc, *scratch):
        side = 1 - s_ref[bit] if away else s_ref[bit]

        def rows_of(i):
            block = (i >> low << (low + 1)) + (side << low) + (i & ((1 << low) - 1))
            return x_ref.at[part(block * LEAF, LEAF)]

        def copy(i):
            held, sem = scratch
            return pltpu.make_async_copy(rows_of(i), held.at[i % 2], sem.at[i % 2])

        if streamed:
            copy(0).start()
        for i in range(TENSOR // 2):
            if streamed:
                if i + 1 < TENSOR // 2:
                    copy(i + 1).start()
                copy(i).wait()
            to = o_ref.at[i * LEAF : (i + 1) * LEAF]
            (acc if away else to)[...] = lax.dot_general(
                (scratch[0].at[i % 2] if streamed else rows_of(i))[...],
                y_ref[:, columns],
                (((1,), (1,)), ((), ())),
                preferred_element_type=jnp.float32,
            )
            if away:

                @pl.loop(0, LEAF // GROUP)
                def _(r):
                    r = part(r * GROUP, GROUP)
                    for c in range(0, n, 128):
                        to[r, c : c + 128] = encode(acc[r, c : c + 128])

    return pl.pallas_call(
        kernel,
        out_shape=pltpu.VMEM((rows, n), jnp.int16 if away else jnp.float32),
        in_specs=[IN_SMEM, IN_HBM if streamed else IN_VMEM, IN_VMEM],
        out_specs=IN_VMEM,
        scratch_shapes=[pltpu.VMEM((LEAF, n), jnp.float32)]
        + streamed * [pltpu.VMEM((2, LEAF, k), x.dtype), pltpu.SemaphoreType.DMA((2,))],
        compiler_params=params(4),
        cost_estimate=BRIEF,
        name="gram",
    )(scalars, pltpu.with_memory_space_constraint(x, pltpu.HBM) if streamed else vmem(x), vmem(y))


def fold(scalars, kept, arrived, bit):
    rows, n = kept.shape
    half = rows // 2

    def kernel(s_ref, kept_ref, in_ref, send_ref, out_ref):
        keep = s_ref[bit]

        @pl.loop(0, half // GROUP)
        def _(r):
            away = part((1 - keep) * half + r * GROUP, GROUP)
            stay = part(keep * half + r * GROUP, GROUP)
            to = part(r * GROUP, GROUP)
            for c in range(0, n, 128):
                c = slice(c, c + 128)
                send_ref[to, c] = encode(kept_ref[away, c] + decode(in_ref[away, c]))
                out_ref[to, c] = kept_ref[stay, c] + decode(in_ref[stay, c])

    return pl.pallas_call(
        kernel,
        out_shape=(pltpu.VMEM((half, n), jnp.int16), pltpu.VMEM((half, n), jnp.float32)),
        in_specs=[IN_SMEM, IN_VMEM, IN_VMEM],
        out_specs=(IN_VMEM, IN_VMEM),
        compiler_params=params(4),
        cost_estimate=BRIEF,
        name="fold",
    )(scalars, vmem(kept), vmem(arrived))


def finish(scalars, act, act_in, grad, grad_in, ids):
    def kernel(s_ref, a_ref, ai_ref, g_ref, gi_ref, ids_ref, col_ref, seq_ref):
        lane = lax.broadcasted_iota(jnp.int32, (GROUP, 128), 1)
        seq = jnp.zeros((1, 128), jnp.float32)
        cols = [jnp.zeros((1, 128), jnp.float32) for _ in range(WAVE // 128)]
        leaf = 4 * s_ref[0] + 2 * s_ref[1] + s_ref[2]
        for r in range(0, LEAF, GROUP):
            rows = slice(r, r + GROUP)
            wide = jnp.zeros((GROUP, 128), jnp.float32)
            for j in range(WAVE // 128):
                c = slice(j * 128, j * 128 + 128)
                ghost = (a_ref[rows, c] + decode(ai_ref[rows, c])) * (g_ref[rows, c] + decode(gi_ref[rows, c]))
                wide = wide + ghost
                cols[j] = cols[j] + jnp.sum(ghost, axis=0, keepdims=True)
            total = jnp.sum(wide, axis=1, keepdims=True)
            mine = ids_ref[part(leaf * LEAF + r, GROUP)] == lane
            seq = seq + jnp.sum(jnp.where(mine, total, 0.0), axis=0, keepdims=True)
        for j in range(WAVE // 128):
            col_ref[:, j * 128 : j * 128 + 128] = cols[j]
        seq_ref[...] = seq

    return pl.pallas_call(
        kernel,
        out_shape=(pltpu.VMEM((1, WAVE), jnp.float32), pltpu.VMEM((1, 128), jnp.float32)),
        in_specs=[IN_SMEM] + [IN_VMEM] * 5,
        out_specs=(IN_VMEM, IN_VMEM),
        compiler_params=params(4),
        cost_estimate=BRIEF,
        name="finish",
    )(scalars, vmem(act), vmem(act_in), vmem(grad), vmem(grad_in), vmem(ids))


def scalar_table():
    table = []
    for d in range(DP):
        for t in range(TENSOR):
            side = ((t // 2 + 1) // 2 % 2, t // 4, t % 2)
            table.append([side[link] for link in LINK_OF_BIT[d % 2]] + [0] + column_order(d))
    return np.array(table, np.int32)


def local(train_hidden, train_grad, val_hidden, val_grad, seq_ids):
    device = lax.axis_index(("dp", "tensor"))
    scalars = lax.dynamic_index_in_dim(jnp.asarray(scalar_table()), device, keepdims=False)
    ids = seq_ids.reshape(TOK_DEV, 1)
    scalars, ids, val_hidden, val_grad = lax.optimization_barrier((scalars, ids, val_hidden, val_grad))
    last = [scalars]

    def after(x):
        return tie(x, last[0])

    def ordered(x):
        last[0] = x
        return x

    def joined(*arrays):
        return ordered(join([after(arrays[0]), *arrays[1:]]))

    def send_half(x, vals, bit):
        send = ordered(gram(scalars, x, after(vals), bit, True))
        return send_link(send, bit)

    def keep_half(x, vals, bit):
        return ordered(gram(scalars, x, after(vals), bit, False))

    def folded(kept, arrived, bit):
        send, kept = fold(scalars, after(kept), arrived, bit)
        ordered(kept)
        return kept, send_link(send, bit)

    own = ordered(beside(after(val_hidden), val_grad))
    near1 = send_dp(own, first_x)
    far0 = send_dp(own, along_z)
    near_pair = joined(own, near1)
    near2 = pieces(near_pair, 2, second_x)
    near_c1 = pieces(near_pair, 2, along_core)
    far0 = joined(far0)
    near_half = joined(near_pair, *near_c1)
    near2 = joined(*near2)
    near_c2 = pieces(near2, 4, along_core)
    far1 = send_dp(after(far0), first_x)
    near = joined(near_half, near2, *near_c2)

    act0_in = send_half(train_hidden, near, 0)
    far_pair = joined(far0, far1)
    far2 = send_dp(far_pair, second_x)
    far_c1 = send_dp(far_pair, along_core)
    grad0_in = send_half(train_grad, near, 2)
    far_half = joined(far_pair, far_c1)
    act0 = keep_half(train_hidden, near, 0)
    grad0 = keep_half(train_grad, near, 2)
    far_rest = both_cores(joined(far2, far2))
    act0, act0_in = folded(act0, act0_in, 1)
    far = joined(far_half, far_rest)
    act1_in = send_half(train_hidden, far, 0)
    grad1_in = send_half(train_grad, far, 2)
    grad0, grad0_in = folded(grad0, grad0_in, 0)
    act1 = keep_half(train_hidden, far, 0)
    grad1 = keep_half(train_grad, far, 2)
    act0, act0_in = folded(act0, act0_in, 2)
    act1, act1_in = folded(act1, act1_in, 1)
    grad0, grad0_in = folded(grad0, grad0_in, 1)
    act1, act1_in = folded(act1, act1_in, 2)
    grad1, grad1_in = folded(grad1, grad1_in, 0)
    grad1, grad1_in = folded(grad1, grad1_in, 1)
    col0, seq0 = finish(scalars, after(act0), act0_in, grad0, grad0_in, ids)
    ordered(col0)
    col1, seq1 = finish(scalars, after(act1), act1_in, grad1, grad1_in, ids)

    ours = (scalars[None, 4:] == jnp.arange(DP, dtype=jnp.int32)[:, None])[:, :, None].astype(jnp.float32)
    col = jnp.concatenate([col0, col1], axis=1).reshape(1, DP, VAL_DEV)
    col = jnp.sum(ours * col, axis=1).reshape(8, 128)
    total = jnp.concatenate([col, seq0 + seq1], axis=0)
    for link in range(3):
        total = total + lax.ppermute(total, "tensor", [(i, along_link(i, link)) for i in range(TENSOR)])
    segment = total[8, :SEQ_DEV]
    total = total[:8]
    for fn in (first_x, second_x):
        total = total + send_dp(total, fn)
    total = total + send_wrap(total)
    total = total + send_dp(total, along_core)
    seq_scale = 1.0 / (float(FF) * D * VAL * TOK_DEV) ** 0.5
    val_scale = 1.0 / (float(FF) * D * TOK_DEV * DP) ** 0.5
    return (segment * seq_scale, total.reshape(VAL) * val_scale)


def solution(mesh):
    in_specs = (
        P("dp", "tensor"),
        P("dp", "tensor"),
        P("dp", "tensor"),
        P("dp", "tensor"),
        P("dp", None),
    )
    out_specs = (P("dp"), P())
    return jax.shard_map(local, mesh=mesh, in_specs=in_specs, out_specs=out_specs, check_vma=False)
```

```python
import jax
import jax.numpy as jnp
import numpy as np
from jax import lax
from jax.experimental import pallas as pl
from jax.experimental.pallas import tpu as pltpu
from jax.sharding import PartitionSpec as P

D = 8192
FF = 28672
TOK_DEV = 2048
SEQ_DEV = 8
VAL = 1024

DP = 16
TENSOR = 8
VAL_DEV = VAL // DP
LEAF = TOK_DEV // TENSOR
WAVE = VAL // 2
HIDDEN_DEV = FF // TENSOR
GRAD_DEV = D // TENSOR
GROUP = 64
BIAS = 100.0
MANTISSA = 16383.0


def along_z(d):
    return (d + 8) % 16


def along_core(d):
    return d ^ 1


def move_x(d, fn):
    z, x, core = d // 8, d // 2 % 4, d % 2
    return z * 8 + fn(x) * 2 + core


def first_x(d):
    return move_x(d, lambda x: x ^ 1 if d % 2 == 0 else 3 - x)


def second_x(d):
    return move_x(d, lambda x: 3 - x if d % 2 == 0 else x ^ 1)


def along_link(t, link):
    y, z = t // 2, t % 2
    if link == 0:
        return (y ^ 1) * 2 + z
    if link == 1:
        return (3 - y) * 2 + z
    return t ^ 1


LINK_OF_BIT = ((0, 1, 2), (1, 0, 2))


def send_dp(x, fn):
    return lax.ppermute(x, "dp", [(d, fn(d)) for d in range(DP)])


def send_link(x, bit):
    pairs = []
    for d in range(DP):
        link = LINK_OF_BIT[d % 2][bit]
        for t in range(TENSOR):
            pairs.append((d * TENSOR + t, d * TENSOR + along_link(t, link)))
    return lax.ppermute(x, ("dp", "tensor"), pairs)


def send_wrap(x):
    pairs = []
    for d in range(DP):
        for t in range(TENSOR):
            pairs.append((d * TENSOR + t, along_z(d) * TENSOR + (t ^ 1)))
    return lax.ppermute(x, ("dp", "tensor"), pairs)


def encode(x):
    a = x.reshape(8, 8, x.shape[-1])
    top = jnp.max(jnp.abs(a), axis=0)
    e = jnp.clip(jnp.floor(jnp.log2(jnp.maximum(top, 1e-26)) + 1.0002), -90.0, 120.0)
    inv = jnp.exp2(-e) * MANTISSA
    code = (e + BIAS).astype(jnp.int32)
    q = jnp.floor(a * inv[None] + 0.5).astype(jnp.int32) * 2
    bits = jnp.stack([(code >> i) & 1 for i in range(8)])
    return (q + bits).reshape(x.shape).astype(jnp.int16)


def decode(c):
    c = c.astype(jnp.int32).reshape(8, 8, c.shape[-1])
    low = c & 1
    code = low[0]
    for i in range(1, 8):
        code = code | (low[i] << i)
    s = jnp.exp2(code.astype(jnp.float32) - BIAS) * (1.0 / MANTISSA)
    return ((c >> 1).astype(jnp.float32) * s[None]).reshape(GROUP, c.shape[-1])


IN_VMEM = pl.BlockSpec(memory_space=pltpu.VMEM)
IN_SMEM = pl.BlockSpec(memory_space=pltpu.SMEM)
BRIEF = pl.CostEstimate(flops=1, bytes_accessed=1, transcendentals=0)


def vmem(x):
    return pltpu.with_memory_space_constraint(x, pltpu.VMEM)


def params(mib):
    return pltpu.CompilerParams(vmem_limit_bytes=mib * 1024 * 1024)


def part(start, size):
    if isinstance(start, int):
        return pl.ds(start, size)
    return pl.ds(pl.multiple_of(start, size), size)


def join(arrays):
    rows = [a.shape[0] for a in arrays]
    n = arrays[0].shape[1]

    def kernel(*refs):
        to = 0
        for ref, size in zip(refs[:-1], rows):
            refs[-1][to : to + size] = ref[...]
            to += size

    return pl.pallas_call(
        kernel,
        out_shape=pltpu.VMEM((sum(rows), n), arrays[0].dtype),
        in_specs=[IN_VMEM] * len(arrays),
        out_specs=IN_VMEM,
        compiler_params=params(4),
        cost_estimate=BRIEF,
        name="join",
    )(*[vmem(a) for a in arrays])


def beside(hidden, grad):
    def kernel(hidden_ref, grad_ref, out_ref):
        out_ref[:, :HIDDEN_DEV] = hidden_ref[...]
        out_ref[:, HIDDEN_DEV:] = grad_ref[...]

    return pl.pallas_call(
        kernel,
        out_shape=pltpu.VMEM((VAL_DEV, HIDDEN_DEV + GRAD_DEV), hidden.dtype),
        in_specs=[IN_VMEM, IN_VMEM],
        out_specs=IN_VMEM,
        compiler_params=params(4),
        cost_estimate=BRIEF,
        name="beside",
    )(vmem(hidden), vmem(grad))


def tie(x, after):
    return lax.optimization_barrier((x, after))[0]


def pieces(rows, count, fn):
    size = rows.shape[0] // count
    return [send_dp(rows[i * size : (i + 1) * size], fn) for i in range(count)]


def both_cores(twice):
    groups = [[d, d + 1] for d in range(0, DP, 2)]
    return lax.all_to_all(twice, "dp", 0, 0, axis_index_groups=groups, tiled=True)


def column_order(d):
    order = []
    for far in (False, True):
        near_part, other_part = [], []
        for e, held in ((d, near_part), (along_core(d), other_part)):
            e = along_z(e) if far else e
            held += [e, first_x(e), second_x(e), first_x(second_x(e))]
        rest = (near_part[2:], other_part[2:])
        rest = rest[:: -1 if far and d % 2 else 1]
        order += near_part[:2] + other_part[:2] + rest[0] + rest[1]
    return order


def tiles(m, n):
    for r in range(0, m, GROUP):
        for c in range(0, n, 128):
            yield r, c


def gram(scalars, x, y, bit, away):
    n, k = y.shape[0], x.shape[1]
    columns = slice(0, HIDDEN_DEV) if k == HIDDEN_DEV else slice(HIDDEN_DEV, HIDDEN_DEV + GRAD_DEV)
    rows = TOK_DEV // 2
    low = 2 - bit

    def kernel(s_ref, x_ref, y_ref, o_ref, acc):
        side = 1 - s_ref[bit] if away else s_ref[bit]
        blocks = TENSOR // 2
        for i in range(blocks + away):
            if i < blocks:
                block = (i >> low << (low + 1)) + (side << low) + (i & ((1 << low) - 1))
                to = acc.at[i % 2] if away else o_ref.at[i * LEAF : (i + 1) * LEAF]
                to[...] = lax.dot_general(
                    x_ref[part(block * LEAF, LEAF)],
                    y_ref[:, columns],
                    (((1,), (1,)), ((), ())),
                    preferred_element_type=jnp.float32,
                )
            if away and i > 0:
                for r, c in tiles(LEAF, n):
                    o_ref[(i - 1) * LEAF + r : (i - 1) * LEAF + r + GROUP, c : c + 128] = encode(
                        acc[(i - 1) % 2, r : r + GROUP, c : c + 128]
                    )

    return pl.pallas_call(
        kernel,
        out_shape=pltpu.VMEM((rows, n), jnp.int16 if away else jnp.float32),
        in_specs=[IN_SMEM, IN_VMEM, IN_VMEM],
        out_specs=IN_VMEM,
        scratch_shapes=[pltpu.VMEM((2, LEAF, n), jnp.float32)] if away else [pltpu.VMEM((8, 128), jnp.float32)],
        compiler_params=params(4),
        cost_estimate=BRIEF,
        name="gram",
    )(scalars, vmem(x), vmem(y))


def fold(scalars, kept, arrived, bit):
    rows, n = kept.shape
    half = rows // 2

    def kernel(s_ref, kept_ref, in_ref, send_ref, out_ref):
        keep = s_ref[bit]

        @pl.loop(0, half // GROUP)
        def _(r):
            away = part((1 - keep) * half + r * GROUP, GROUP)
            stay = part(keep * half + r * GROUP, GROUP)
            to = part(r * GROUP, GROUP)
            for c in range(0, n, 128):
                c = slice(c, c + 128)
                send_ref[to, c] = encode(kept_ref[away, c] + decode(in_ref[away, c]))
                out_ref[to, c] = kept_ref[stay, c] + decode(in_ref[stay, c])

    return pl.pallas_call(
        kernel,
        out_shape=(pltpu.VMEM((half, n), jnp.int16), pltpu.VMEM((half, n), jnp.float32)),
        in_specs=[IN_SMEM, IN_VMEM, IN_VMEM],
        out_specs=(IN_VMEM, IN_VMEM),
        compiler_params=params(4),
        cost_estimate=BRIEF,
        name="fold",
    )(scalars, vmem(kept), vmem(arrived))


def finish(scalars, act, act_in, grad, grad_in, ids):
    def kernel(s_ref, a_ref, ai_ref, g_ref, gi_ref, ids_ref, col_ref, seq_ref):
        lane = lax.broadcasted_iota(jnp.int32, (GROUP, 128), 1)
        seq = jnp.zeros((1, 128), jnp.float32)
        cols = [jnp.zeros((1, 128), jnp.float32) for _ in range(WAVE // 128)]
        leaf = 4 * s_ref[0] + 2 * s_ref[1] + s_ref[2]
        ids = ids_ref[...]
        first = jnp.zeros((1, 128), jnp.int32)
        past = jnp.zeros((1, 128), jnp.int32)
        for q in range(SEQ_DEV):
            first = jnp.where(lane[:1] == q, jnp.sum((ids < q).astype(jnp.int32), axis=1, keepdims=True), first)
            past = jnp.where(lane[:1] == q, jnp.sum((ids <= q).astype(jnp.int32), axis=1, keepdims=True), past)
        for r in range(0, LEAF, GROUP):
            rows = slice(r, r + GROUP)
            wide = jnp.zeros((GROUP, 128), jnp.float32)
            for j in range(WAVE // 128):
                c = slice(j * 128, j * 128 + 128)
                ghost = (a_ref[rows, c] + decode(ai_ref[rows, c])) * (g_ref[rows, c] + decode(gi_ref[rows, c]))
                wide = wide + ghost
                cols[j] = cols[j] + jnp.sum(ghost, axis=0, keepdims=True)
            total = jnp.sum(wide, axis=1, keepdims=True)
            token = leaf * LEAF + r + lax.broadcasted_iota(jnp.int32, (GROUP, 128), 0)
            mine = (token >= first) & (token < past)
            seq = seq + jnp.sum(jnp.where(mine, total, 0.0), axis=0, keepdims=True)
        for j in range(WAVE // 128):
            col_ref[:, j * 128 : j * 128 + 128] = cols[j]
        seq_ref[...] = seq

    return pl.pallas_call(
        kernel,
        out_shape=(pltpu.VMEM((1, WAVE), jnp.float32), pltpu.VMEM((1, 128), jnp.float32)),
        in_specs=[IN_SMEM] + [IN_VMEM] * 5,
        out_specs=(IN_VMEM, IN_VMEM),
        compiler_params=params(4),
        cost_estimate=BRIEF,
        name="finish",
    )(scalars, vmem(act), vmem(act_in), vmem(grad), vmem(grad_in), vmem(ids))


def scalar_table():
    table = []
    for d in range(DP):
        for t in range(TENSOR):
            side = ((t // 2 + 1) // 2 % 2, t // 4, t % 2)
            table.append([side[link] for link in LINK_OF_BIT[d % 2]] + [0] + column_order(d))
    return np.array(table, np.int32)


def local(train_hidden, train_grad, val_hidden, val_grad, seq_ids):
    device = lax.axis_index(("dp", "tensor"))
    scalars = lax.dynamic_index_in_dim(jnp.asarray(scalar_table()), device, keepdims=False)
    scalars, val_hidden, val_grad = lax.optimization_barrier((scalars, val_hidden, val_grad))
    last = [scalars]

    def after(x):
        return tie(x, last[0])

    def ordered(x):
        last[0] = x
        return x

    def joined(*arrays):
        return ordered(join([after(arrays[0]), *arrays[1:]]))

    def send_half(x, vals, bit):
        send = ordered(gram(scalars, x, after(vals), bit, True))
        return send_link(send, bit)

    def keep_half(x, vals, bit):
        return ordered(gram(scalars, x, after(vals), bit, False))

    def folded(kept, arrived, bit):
        send, kept = fold(scalars, after(kept), arrived, bit)
        ordered(kept)
        return kept, send_link(send, bit)

    own = ordered(beside(after(val_hidden), val_grad))
    near1 = send_dp(own, first_x)
    far0 = send_dp(own, along_z)
    near_pair = joined(own, near1)
    near2 = pieces(near_pair, 2, second_x)
    near_c1 = pieces(near_pair, 2, along_core)
    far0 = joined(far0)
    near_half = joined(near_pair, *near_c1)
    near2 = joined(*near2)
    near_c2 = pieces(near2, 4, along_core)
    far1 = send_dp(after(far0), first_x)
    near = joined(near_half, near2, *near_c2)

    act0_in = send_half(train_hidden, near, 0)
    far_pair = joined(far0, far1)
    far2 = send_dp(far_pair, second_x)
    far_c1 = send_dp(far_pair, along_core)
    grad0_in = send_half(train_grad, near, 2)
    far_half = joined(far_pair, far_c1)
    act0 = keep_half(train_hidden, near, 0)
    grad0 = keep_half(train_grad, near, 2)
    far_rest = both_cores(joined(far2, far2))
    act0, act0_in = folded(act0, act0_in, 1)
    far = joined(far_half, far_rest)
    act1_in = send_half(train_hidden, far, 0)
    grad1_in = send_half(train_grad, far, 2)
    grad0, grad0_in = folded(grad0, grad0_in, 0)
    act1 = keep_half(train_hidden, far, 0)
    grad1 = keep_half(train_grad, far, 2)
    act1, act1_in = folded(act1, act1_in, 1)
    grad1, grad1_in = folded(grad1, grad1_in, 0)
    act0, act0_in = folded(act0, act0_in, 2)
    grad0, grad0_in = folded(grad0, grad0_in, 1)
    act1, act1_in = folded(act1, act1_in, 2)
    grad1, grad1_in = folded(grad1, grad1_in, 1)
    col0, seq0 = finish(scalars, after(act0), act0_in, grad0, grad0_in, seq_ids)
    ordered(col0)
    col1, seq1 = finish(scalars, after(act1), act1_in, grad1, grad1_in, seq_ids)

    ours = (scalars[None, 4:] == jnp.arange(DP, dtype=jnp.int32)[:, None])[:, :, None].astype(jnp.float32)
    col = jnp.concatenate([col0, col1], axis=1).reshape(1, DP, VAL_DEV)
    col = jnp.sum(ours * col, axis=1).reshape(8, 128)
    total = jnp.concatenate([col, seq0 + seq1], axis=0)
    for link in range(3):
        total = total + lax.ppermute(total, "tensor", [(i, along_link(i, link)) for i in range(TENSOR)])
    segment = total[8, :SEQ_DEV]
    total = total[:8]
    for fn in (first_x, second_x):
        total = total + send_dp(total, fn)
    total = total + send_wrap(total)
    total = total + send_dp(total, along_core)
    seq_scale = 1.0 / (float(FF) * D * VAL * TOK_DEV) ** 0.5
    val_scale = 1.0 / (float(FF) * D * TOK_DEV * DP) ** 0.5
    return (segment * seq_scale, total.reshape(VAL) * val_scale)


def solution(mesh):
    in_specs = (
        P("dp", "tensor"),
        P("dp", "tensor"),
        P("dp", "tensor"),
        P("dp", "tensor"),
        P("dp", None),
    )
    out_specs = (P("dp"), P())
    return jax.shard_map(local, mesh=mesh, in_specs=in_specs, out_specs=out_specs, check_vma=False)
```

```python
import jax
import jax.numpy as jnp
import numpy as np
from jax import lax
from jax.experimental import pallas as pl
from jax.experimental.pallas import tpu as pltpu
from jax.sharding import PartitionSpec as P

D = 8192
FF = 28672
TOK_DEV = 2048
SEQ_DEV = 8
VAL = 1024

DP = 16
TENSOR = 8
VAL_DEV = VAL // DP
LEAF = TOK_DEV // TENSOR
WAVE = VAL // 2
HIDDEN_DEV = FF // TENSOR
GRAD_DEV = D // TENSOR
GROUP = 64
BIAS = 100.0
MANTISSA = 16383.0


def along_z(d):
    return (d + 8) % 16


def along_core(d):
    return d ^ 1


def move_x(d, fn):
    z, x, core = d // 8, d // 2 % 4, d % 2
    return z * 8 + fn(x) * 2 + core


def first_x(d):
    return move_x(d, lambda x: x ^ 1 if d % 2 == 0 else 3 - x)


def second_x(d):
    return move_x(d, lambda x: 3 - x if d % 2 == 0 else x ^ 1)


def along_link(t, link):
    y, z = t // 2, t % 2
    if link == 0:
        return (y ^ 1) * 2 + z
    if link == 1:
        return (3 - y) * 2 + z
    return t ^ 1


LINK_OF_BIT = ((0, 1, 2), (1, 0, 2))


def send_dp(x, fn):
    return lax.ppermute(x, "dp", [(d, fn(d)) for d in range(DP)])


def send_link(x, bit):
    pairs = []
    for d in range(DP):
        link = LINK_OF_BIT[d % 2][bit]
        for t in range(TENSOR):
            pairs.append((d * TENSOR + t, d * TENSOR + along_link(t, link)))
    return lax.ppermute(x, ("dp", "tensor"), pairs)


def send_wrap(x):
    pairs = []
    for d in range(DP):
        for t in range(TENSOR):
            pairs.append((d * TENSOR + t, along_z(d) * TENSOR + (t ^ 1)))
    return lax.ppermute(x, ("dp", "tensor"), pairs)


def encode(x):
    a = x.reshape(8, 8, x.shape[-1])
    top = jnp.max(jnp.abs(a), axis=0)
    e = jnp.clip(jnp.floor(jnp.log2(jnp.maximum(top, 1e-26)) + 1.0002), -90.0, 120.0)
    inv = jnp.exp2(-e) * MANTISSA
    code = (e + BIAS).astype(jnp.int32)
    q = jnp.floor(a * inv[None] + 0.5).astype(jnp.int32) * 2
    bits = jnp.stack([(code >> i) & 1 for i in range(8)])
    return (q + bits).reshape(x.shape).astype(jnp.int16)


def decode(c):
    c = c.astype(jnp.int32).reshape(8, 8, c.shape[-1])
    low = c & 1
    code = low[0]
    for i in range(1, 8):
        code = code | (low[i] << i)
    s = jnp.exp2(code.astype(jnp.float32) - BIAS) * (1.0 / MANTISSA)
    return ((c >> 1).astype(jnp.float32) * s[None]).reshape(GROUP, c.shape[-1])


IN_VMEM = pl.BlockSpec(memory_space=pltpu.VMEM)
IN_SMEM = pl.BlockSpec(memory_space=pltpu.SMEM)
IN_HBM = pl.BlockSpec(memory_space=pltpu.HBM)
BRIEF = pl.CostEstimate(flops=1, bytes_accessed=1, transcendentals=0)


def vmem(x):
    return pltpu.with_memory_space_constraint(x, pltpu.VMEM)


def params(mib):
    return pltpu.CompilerParams(vmem_limit_bytes=mib * 1024 * 1024)


def part(start, size):
    if isinstance(start, int):
        return pl.ds(start, size)
    return pl.ds(pl.multiple_of(start, size), size)


def join(arrays):
    rows = [a.shape[0] for a in arrays]
    n = arrays[0].shape[1]

    def kernel(*refs):
        to = 0
        for ref, size in zip(refs[:-1], rows):
            refs[-1][to : to + size] = ref[...]
            to += size

    return pl.pallas_call(
        kernel,
        out_shape=pltpu.VMEM((sum(rows), n), arrays[0].dtype),
        in_specs=[IN_VMEM] * len(arrays),
        out_specs=IN_VMEM,
        compiler_params=params(4),
        cost_estimate=BRIEF,
        name="join",
    )(*[vmem(a) for a in arrays])


def beside(hidden, grad):
    def kernel(hidden_ref, grad_ref, out_ref, sem):
        copies = [
            pltpu.make_async_copy(hidden_ref, out_ref.at[:, :HIDDEN_DEV], sem.at[0]),
            pltpu.make_async_copy(grad_ref, out_ref.at[:, HIDDEN_DEV:], sem.at[1]),
        ]
        for copy in copies:
            copy.start()
        for copy in copies:
            copy.wait()

    return pl.pallas_call(
        kernel,
        out_shape=pltpu.VMEM((VAL_DEV, HIDDEN_DEV + GRAD_DEV), hidden.dtype),
        in_specs=[IN_HBM, IN_HBM],
        out_specs=IN_VMEM,
        scratch_shapes=[pltpu.SemaphoreType.DMA((2,))],
        compiler_params=params(1),
        cost_estimate=BRIEF,
        name="beside",
    )(*[pltpu.with_memory_space_constraint(a, pltpu.HBM) for a in (hidden, grad)])


def tie(x, after):
    return lax.optimization_barrier((x, after))[0]


def pieces(rows, count, fn):
    size = rows.shape[0] // count
    return [send_dp(rows[i * size : (i + 1) * size], fn) for i in range(count)]


def both_cores(twice):
    groups = [[d, d + 1] for d in range(0, DP, 2)]
    return lax.all_to_all(twice, "dp", 0, 0, axis_index_groups=groups, tiled=True)


def column_order(d):
    order = []
    for far in (False, True):
        near_part, other_part = [], []
        for e, held in ((d, near_part), (along_core(d), other_part)):
            e = along_z(e) if far else e
            held += [e, first_x(e), second_x(e), first_x(second_x(e))]
        rest = (near_part[2:], other_part[2:])
        rest = rest[:: -1 if far and d % 2 else 1]
        order += near_part[:2] + other_part[:2] + rest[0] + rest[1]
    return order


def tiles(m, n):
    for r in range(0, m, GROUP):
        for c in range(0, n, 128):
            yield r, c


def gram(scalars, x, y, bit, away):
    n, k = y.shape[0], x.shape[1]
    columns = slice(0, HIDDEN_DEV) if k == HIDDEN_DEV else slice(HIDDEN_DEV, HIDDEN_DEV + GRAD_DEV)
    rows = TOK_DEV // 2
    low = 2 - bit

    def kernel(s_ref, x_ref, y_ref, o_ref, acc):
        side = 1 - s_ref[bit] if away else s_ref[bit]
        blocks = TENSOR // 2
        for i in range(blocks + away):
            if i < blocks:
                block = (i >> low << (low + 1)) + (side << low) + (i & ((1 << low) - 1))
                to = acc.at[i % 2] if away else o_ref.at[i * LEAF : (i + 1) * LEAF]
                to[...] = lax.dot_general(
                    x_ref[part(block * LEAF, LEAF)],
                    y_ref[:, columns],
                    (((1,), (1,)), ((), ())),
                    preferred_element_type=jnp.float32,
                )
            if away and i > 0:
                for r, c in tiles(LEAF, n):
                    o_ref[(i - 1) * LEAF + r : (i - 1) * LEAF + r + GROUP, c : c + 128] = encode(
                        acc[(i - 1) % 2, r : r + GROUP, c : c + 128]
                    )

    return pl.pallas_call(
        kernel,
        out_shape=pltpu.VMEM((rows, n), jnp.int16 if away else jnp.float32),
        in_specs=[IN_SMEM, IN_VMEM, IN_VMEM],
        out_specs=IN_VMEM,
        scratch_shapes=[pltpu.VMEM((2, LEAF, n), jnp.float32)] if away else [pltpu.VMEM((8, 128), jnp.float32)],
        compiler_params=params(4),
        cost_estimate=BRIEF,
        name="gram",
    )(scalars, vmem(x), vmem(y))


def fold(scalars, kept, arrived, bit, run=None):
    rows, n = kept.shape
    half = rows // 2
    run = run or half

    def kernel(s_ref, kept_ref, in_ref, send_ref, out_ref):
        keep = s_ref[bit]

        @pl.loop(0, half // GROUP)
        def _(r):
            row = r * GROUP
            base = row // run * 2 * run + row % run
            away = part(base + (1 - keep) * run, GROUP)
            stay = part(base + keep * run, GROUP)
            to = part(r * GROUP, GROUP)
            for c in range(0, n, 128):
                c = slice(c, c + 128)
                send_ref[to, c] = encode(kept_ref[away, c] + decode(in_ref[away, c]))
                out_ref[to, c] = kept_ref[stay, c] + decode(in_ref[stay, c])

    return pl.pallas_call(
        kernel,
        out_shape=(pltpu.VMEM((half, n), jnp.int16), pltpu.VMEM((half, n), jnp.float32)),
        in_specs=[IN_SMEM, IN_VMEM, IN_VMEM],
        out_specs=(IN_VMEM, IN_VMEM),
        compiler_params=params(4),
        cost_estimate=BRIEF,
        name="fold",
    )(scalars, vmem(kept), vmem(arrived))


def finish(scalars, act, act_in, grad, grad_in, ids):
    def kernel(s_ref, a_ref, ai_ref, g_ref, gi_ref, ids_ref, col_ref, seq_ref):
        lane = lax.broadcasted_iota(jnp.int32, (GROUP, 128), 1)
        seq = jnp.zeros((1, 128), jnp.float32)
        cols = [jnp.zeros((1, 128), jnp.float32) for _ in range(WAVE // 128)]
        leaf = 4 * s_ref[0] + 2 * s_ref[1] + s_ref[2]
        ids = ids_ref[...]
        first = jnp.zeros((1, 128), jnp.int32)
        past = jnp.zeros((1, 128), jnp.int32)
        for q in range(SEQ_DEV):
            first = jnp.where(lane[:1] == q, jnp.sum((ids < q).astype(jnp.int32), axis=1, keepdims=True), first)
            past = jnp.where(lane[:1] == q, jnp.sum((ids <= q).astype(jnp.int32), axis=1, keepdims=True), past)
        for r in range(0, LEAF, GROUP):
            rows = slice(r, r + GROUP)
            wide = jnp.zeros((GROUP, 128), jnp.float32)
            for j in range(WAVE // 128):
                c = slice(j * 128, j * 128 + 128)
                ghost = (a_ref[rows, c] + decode(ai_ref[rows, c])) * (g_ref[rows, c] + decode(gi_ref[rows, c]))
                wide = wide + ghost
                cols[j] = cols[j] + jnp.sum(ghost, axis=0, keepdims=True)
            total = jnp.sum(wide, axis=1, keepdims=True)
            token = leaf * LEAF + r + lax.broadcasted_iota(jnp.int32, (GROUP, 128), 0)
            mine = (token >= first) & (token < past)
            seq = seq + jnp.sum(jnp.where(mine, total, 0.0), axis=0, keepdims=True)
        for j in range(WAVE // 128):
            col_ref[:, j * 128 : j * 128 + 128] = cols[j]
        seq_ref[...] = seq

    return pl.pallas_call(
        kernel,
        out_shape=(pltpu.VMEM((1, WAVE), jnp.float32), pltpu.VMEM((1, 128), jnp.float32)),
        in_specs=[IN_SMEM] + [IN_VMEM] * 5,
        out_specs=(IN_VMEM, IN_VMEM),
        compiler_params=params(4),
        cost_estimate=BRIEF,
        name="finish",
    )(scalars, vmem(act), vmem(act_in), vmem(grad), vmem(grad_in), vmem(ids))


def scalar_table():
    table = []
    for d in range(DP):
        for t in range(TENSOR):
            side = ((t // 2 + 1) // 2 % 2, t // 4, t % 2)
            table.append([side[link] for link in LINK_OF_BIT[d % 2]] + [0] + column_order(d))
    return np.array(table, np.int32)


def local(train_hidden, train_grad, val_hidden, val_grad, seq_ids):
    device = lax.axis_index(("dp", "tensor"))
    scalars = lax.dynamic_index_in_dim(jnp.asarray(scalar_table()), device, keepdims=False)
    scalars, val_hidden, val_grad = lax.optimization_barrier((scalars, val_hidden, val_grad))
    last = [scalars]

    def after(x):
        return tie(x, last[0])

    def ordered(x):
        last[0] = x
        return x

    def joined(*arrays):
        return ordered(join([after(arrays[0]), *arrays[1:]]))

    def send_half(x, vals, bit):
        send = ordered(gram(scalars, x, after(vals), bit, True))
        return send_link(send, bit)

    def keep_half(x, vals, bit):
        return ordered(gram(scalars, x, after(vals), bit, False))

    def folded(kept, arrived, bit, run=None):
        send, kept = fold(scalars, after(kept), arrived, bit, run)
        ordered(kept)
        return kept, send_link(send, bit)

    own = ordered(beside(after(val_hidden), val_grad))
    near1 = send_dp(own, first_x)
    far0 = send_dp(own, along_z)
    near_pair = joined(own, near1)
    near2 = pieces(near_pair, 2, second_x)
    near_c1 = pieces(near_pair, 2, along_core)
    far0 = joined(far0)
    near_half = joined(near_pair, *near_c1)
    near2 = joined(*near2)
    near_c2 = pieces(near2, 1, along_core)
    far1 = send_dp(after(far0), first_x)
    near = joined(near_half, near2, *near_c2)

    act0_in = send_half(train_hidden, near, 0)
    far_pair = joined(far0, far1)
    far2 = send_dp(far_pair, second_x)
    far_c1 = send_dp(far_pair, along_core)
    grad0_in = send_half(train_grad, near, 2)
    far_half = joined(far_pair, far_c1)
    act0 = keep_half(train_hidden, near, 0)
    grad0 = keep_half(train_grad, near, 2)
    far_rest = both_cores(joined(far2, far2))
    act0, act0_in = folded(act0, act0_in, 1)
    far = joined(far_half, far_rest)
    grad1_in = send_half(train_grad, far, 2)
    act1_in = send_half(train_hidden, far, 0)
    grad0, grad0_in = folded(grad0, grad0_in, 0)
    act1 = keep_half(train_hidden, far, 0)
    grad1 = keep_half(train_grad, far, 2)
    grad1, grad1_in = folded(grad1, grad1_in, 0)
    act1, act1_in = folded(act1, act1_in, 2, LEAF)
    act0, act0_in = folded(act0, act0_in, 2)
    grad0, grad0_in = folded(grad0, grad0_in, 1)
    grad1, grad1_in = folded(grad1, grad1_in, 1)
    act1, act1_in = folded(act1, act1_in, 1)
    last[0] = (last[0], grad1_in)
    col0, seq0 = finish(scalars, after(act0), act0_in, grad0, grad0_in, seq_ids)
    ordered(col0)
    col1, seq1 = finish(scalars, after(act1), act1_in, grad1, grad1_in, seq_ids)

    ours = (scalars[None, 4:] == jnp.arange(DP, dtype=jnp.int32)[:, None])[:, :, None].astype(jnp.float32)
    col = jnp.concatenate([col0, col1], axis=1).reshape(1, DP, VAL_DEV)
    col = jnp.sum(ours * col, axis=1).reshape(8, 128)
    total = jnp.concatenate([col, seq0 + seq1], axis=0)
    for link in range(3):
        total = total + lax.ppermute(total, "tensor", [(i, along_link(i, link)) for i in range(TENSOR)])
    segment = total[8, :SEQ_DEV]
    total = total[:8]
    for fn in (first_x, second_x):
        total = total + send_dp(total, fn)
    total = total + send_wrap(total)
    total = total + send_dp(total, along_core)
    seq_scale = 1.0 / (float(FF) * D * VAL * TOK_DEV) ** 0.5
    val_scale = 1.0 / (float(FF) * D * TOK_DEV * DP) ** 0.5
    return (segment * seq_scale, total.reshape(VAL) * val_scale)


def solution(mesh):
    in_specs = (
        P("dp", "tensor"),
        P("dp", "tensor"),
        P("dp", "tensor"),
        P("dp", "tensor"),
        P("dp", None),
    )
    out_specs = (P("dp"), P())
    return jax.shard_map(local, mesh=mesh, in_specs=in_specs, out_specs=out_specs, check_vma=False)
```
